128 devices in a mesh: tm: 8 (over x, y_lo), row: 8 (over z, y_hi), col: 2 (over core).
Axes of the slice: x: 4, y: 4 (y_hi: 2, y_lo: 2; y = y_hi * 2 + y_lo), z: 4, core: 2. Of those that a mesh axis runs over, the one named last changes fastest.
Arguments:
- tokens: float32 [8, 256, 128, 384], P('tm', 'row', 'col'), may hold values from -6 to 6
- spatial_norm: float32 [384], replicated, may hold values from 0.1 to 1.9
- spatial_qkv: float32 [384, 1152], replicated, may hold values from -1.5 to 1.5
- spatial_out: float32 [384, 384], replicated, may hold values from -0.3125 to 0.3125
- spatial_mlpnorm: float32 [384], replicated, may hold values from 0.1 to 1.9
- spatial_up: float32 [384, 1536], replicated, may hold values from -0.3125 to 0.3125
- spatial_down: float32 [1536, 384], replicated, may hold values from -0.15625 to 0.15625
- temporal_norm: float32 [384], replicated, may hold values from 0.1 to 1.9
- temporal_qkv: float32 [384, 1152], replicated, may hold values from -1.5 to 1.5
- temporal_out: float32 [384, 384], replicated, may hold values from -0.3125 to 0.3125
- temporal_mlpnorm: float32 [384], replicated, may hold values from 0.1 to 1.9
- temporal_up: float32 [384, 1536], replicated, may hold values from -0.3125 to 0.3125
- temporal_down: float32 [1536, 384], replicated, may hold values from -0.15625 to 0.15625
Outputs:
- result: float32 [8, 256, 128, 384], P('tm', 'row', 'col')
The draws below stay inside these ranges and needn't reach their ends.
All inputs are finite; a program needn't handle non-finite values.
Results may differ from the reference program's by a relative error of at most 0.0003.
Values sent between devices are 32-bit elements; how exact they have to be, the bound alone decides.
No kernel may reach another device: no remote copies, remote signals or barrier semaphores. Data moves between devices by JAX's collectives and lax.ppermute only.
A program may use at most 256 MiB of HBM per device.

```python
import math
import jax
import jax.numpy as jnp
from jax import lax

HEADS = 12
HDIM = 32
D = 384
MLP = 1536
WIN = 8
FRAMES = 8
ROWS = 256
COLS = 128


def head_scaled(entries, key):
    order = jax.random.permutation(key, HEADS).astype(jnp.float32)
    factors = 1.0 + 5.0 * order / max(HEADS - 1, 1)
    columns = jnp.arange(3 * D)
    head_of = columns % D // HDIM
    column_factor = jnp.where(columns < 2 * D, factors[head_of], 1.0)
    return jnp.clip(entries * column_factor[None, :] / jnp.sqrt(jnp.float32(D)), -1.5, 1.5)


def draw_spatial_qkv(key, part):
    key = jax.random.fold_in(key, 11)
    first, second = jax.random.split(key)
    entries = jnp.clip(jax.random.normal(first, (D, 3 * D), jnp.float32), -4.0, 4.0)
    return head_scaled(entries, second)


def draw_temporal_qkv(key, part):
    key = jax.random.fold_in(key, 23)
    first, second = jax.random.split(key)
    entries = jnp.clip(jax.random.normal(first, (D, 3 * D), jnp.float32), -4.0, 4.0)
    return head_scaled(entries, second)


def block_scale(key, shape, cuts, smallest, largest):
    factor_of = 1.0
    for dim, parts in cuts:
        draws = jax.random.uniform(jax.random.fold_in(jax.random.fold_in(key, 6), dim), (parts,), jnp.float32, smallest / len(cuts), largest / len(cuts))
        factor_of = factor_of * jnp.repeat(jnp.exp(draws), shape[dim] // parts).reshape((-1,) + (1,) * (len(shape) - 1 - dim))
    return factor_of


def gaussian(own_key, shape, scale, bound, cuts=(), kind=jnp.bfloat16):
    level = block_scale(own_key, shape, cuts, -0.22, 0.18) if cuts else 1.0
    result = jax.random.normal(own_key, shape, jnp.float32) * scale * level
    return jnp.minimum(jnp.maximum(result, -bound), bound).astype(kind)


def setup_inputs(seed: int = 0) -> dict:
    arg_keys = jax.random.split(jax.random.key(seed), 14)
    return {
        "tokens": gaussian(arg_keys[0], (FRAMES, ROWS, COLS, D), 1.0, 6.0, ((0, 8), (1, 8), (2, 2)), jnp.float32),
        "spatial_norm": jnp.clip(1.0 + 0.18 * jax.random.normal(arg_keys[1], (D,), jnp.float32), 0.1, 1.9),
        "spatial_qkv": draw_spatial_qkv(jax.random.fold_in(arg_keys[13], 71), 0),
        "spatial_out": gaussian(arg_keys[3], (D, D), D ** -0.5, 0.3125, (), jnp.float32),
        "spatial_mlpnorm": jnp.clip(1.0 + 0.18 * jax.random.normal(arg_keys[4], (D,), jnp.float32), 0.1, 1.9),
        "spatial_up": gaussian(arg_keys[5], (D, MLP), D ** -0.5, 0.3125, (), jnp.float32),
        "spatial_down": gaussian(arg_keys[6], (MLP, D), MLP ** -0.5, 0.15625, (), jnp.float32),
        "temporal_norm": jnp.clip(1.0 + 0.18 * jax.random.normal(arg_keys[7], (D,), jnp.float32), 0.1, 1.9),
        "temporal_qkv": draw_temporal_qkv(jax.random.fold_in(arg_keys[13], 71), 0),
        "temporal_out": gaussian(arg_keys[9], (D, D), D ** -0.5, 0.3125, (), jnp.float32),
        "temporal_mlpnorm": jnp.clip(1.0 + 0.18 * jax.random.normal(arg_keys[10], (D,), jnp.float32), 0.1, 1.9),
        "temporal_up": gaussian(arg_keys[11], (D, MLP), D ** -0.5, 0.3125, (), jnp.float32),
        "temporal_down": gaussian(arg_keys[12], (MLP, D), MLP ** -0.5, 0.15625, (), jnp.float32),
    }


EPSILON = 1e-05
SOFTCAP = 20.0
PRECISE = lax.Precision.HIGHEST

def layer_norm(inputs, scales):
    average = lax.optimization_barrier(jnp.mean(inputs, axis=-1, keepdims=True))
    centred = inputs - average
    spread = lax.optimization_barrier(jnp.mean(centred * centred, axis=-1, keepdims=True))
    return centred * lax.rsqrt(spread + EPSILON) * scales

def project(inputs, matrix):
    return jnp.einsum('...d,de->...e', inputs, matrix, precision=PRECISE)

def feed_forward(stream, scales, weight_up, weight_down):
    hidden = jax.nn.gelu(project(layer_norm(stream, scales), weight_up), approximate=True)
    return stream + project(hidden, weight_down)

def attend(queries, key_rows, values, allowed):
    scores = jnp.einsum('...qhd,...khd->...hqk', queries, key_rows, precision=PRECISE) / math.sqrt(queries.shape[-1])
    weights = jnp.exp(SOFTCAP * jnp.tanh(scores / SOFTCAP)) * allowed
    totals = lax.optimization_barrier(jnp.sum(weights, axis=-1, keepdims=True))
    totals = jnp.where(totals > 0.0, totals, 1.0)
    return jnp.einsum('...hqk,...khd->...qhd', weights / totals, values, precision=PRECISE)

def to_windows(field_grid):
    frame_n, row_n, col_n, chan_n = field_grid.shape
    field_grid = field_grid.reshape(frame_n, row_n // WIN, WIN, col_n // WIN, WIN, chan_n)
    field_grid = field_grid.transpose(0, 1, 3, 2, 4, 5)
    return field_grid.reshape(frame_n, row_n // WIN, col_n // WIN, WIN * WIN, chan_n)

def from_windows(blocks, row_n, col_n):
    frame_n, across_r, across_c, cells, chan_n = blocks.shape
    blocks = blocks.reshape(frame_n, across_r, across_c, WIN, WIN, chan_n).transpose(0, 1, 3, 2, 4, 5)
    return blocks.reshape(frame_n, row_n, col_n, chan_n)

def window_attention(queries, key_rows, values, inside):
    frame_n, row_n, col_n, channels = queries.shape
    head_count = channels // HDIM
    wq = to_windows(queries)
    wk = to_windows(key_rows)
    wv = to_windows(values)
    shape_heads = wq.shape[:4] + (head_count, HDIM)
    masked = to_windows(inside[None, :, :, None])[..., 0]
    allowed = masked[:, :, :, None, None, :]
    mixture = attend(wq.reshape(shape_heads), wk.reshape(shape_heads), wv.reshape(shape_heads), allowed)
    return from_windows(mixture.reshape(wq.shape), row_n, col_n)

def spatial_frame(stream, gain_attn, weight_qkv, weight_out, gain_mlp, weight_up, weight_down):
    frame_n, row_n, col_n, channels = stream.shape
    half_win = WIN // 2
    projected = project(layer_norm(stream, gain_attn), weight_qkv)
    padded = jnp.pad(projected, ((0, 0), (half_win, half_win), (half_win, half_win), (0, 0)))
    inside = jnp.pad(jnp.ones((row_n, col_n), jnp.float32), half_win)
    mixture = window_attention(padded[..., :channels], padded[..., channels:2 * channels], padded[..., 2 * channels:], inside)
    mixture = mixture[:, half_win:half_win + row_n, half_win:half_win + col_n]
    stream = stream + project(mixture, weight_out)
    return feed_forward(stream, gain_mlp, weight_up, weight_down)

def causal_attention(projected):
    frame_n, place_n, triple = projected.shape
    channels = triple // 3
    head_count = channels // HDIM

    def heads_of(part):
        return part.reshape(frame_n, place_n, head_count, HDIM).transpose(1, 0, 2, 3)
    frame_order = jnp.arange(frame_n)
    allowed = (frame_order[None, :] <= frame_order[:, None]).astype(projected.dtype)
    mixture = attend(heads_of(projected[..., :channels]), heads_of(projected[..., channels:2 * channels]), heads_of(projected[..., 2 * channels:]), allowed)
    return mixture.transpose(1, 0, 2, 3).reshape(frame_n, place_n, channels)

def reference(tokens, spatial_norm, spatial_qkv, spatial_out, spatial_mlpnorm, spatial_up, spatial_down, temporal_norm, temporal_qkv, temporal_out, temporal_mlpnorm, temporal_up, temporal_down):

    def one_frame(frame):
        return spatial_frame(frame[None], spatial_norm, spatial_qkv, spatial_out, spatial_mlpnorm, spatial_up, spatial_down)[0]
    stream = lax.map(one_frame, tokens)
    frame_n, row_n, col_n, channels = stream.shape
    flat_rows = stream.reshape(frame_n, row_n * col_n, channels)
    projected = project(layer_norm(flat_rows, temporal_norm), temporal_qkv)
    flat_rows = flat_rows + project(causal_attention(projected), temporal_out)
    flat_rows = feed_forward(flat_rows, temporal_mlpnorm, temporal_up, temporal_down)
    return flat_rows.reshape(frame_n, row_n, col_n, channels)
```

```python
import functools
import math

import jax
import jax.numpy as jnp
from jax import lax
from jax.experimental import pallas as pl
from jax.experimental.pallas import tpu as pltpu
from jax.sharding import PartitionSpec as P

HDIM = 32
WIN = 8
HALF = WIN // 2
EPSILON = 1e-05
SOFTCAP = 20.0
GROUP = 128
PACK = GROUP // HDIM
CELLS = WIN * WIN
SCORE_SCALE = 1.0 / (SOFTCAP * math.sqrt(HDIM))
EXP_SCALE = SOFTCAP * math.log2(math.e)
GELU_A = math.sqrt(2.0 / math.pi)
GELU_B = 0.044715 * GELU_A
BF16 = jnp.bfloat16
F32 = jnp.float32


def halves(value):
    high = value.astype(BF16)
    low = (value - high.astype(F32)).astype(BF16)
    return high, low


def dot(left, right, contract=((1,), (0,))):
    return lax.dot_general(left, right, (contract, ((), ())), preferred_element_type=F32)


def dot3(value, weight_high, weight_low):
    high, low = halves(value)
    left = jnp.concatenate([high, low, high], axis=1)
    right = jnp.concatenate([weight_high, weight_high, weight_low], axis=0)
    return dot(left, right)


def layer_norm(inputs, scales):
    average = jnp.mean(inputs, axis=-1, keepdims=True)
    centred = inputs - average
    spread = jnp.mean(centred * centred, axis=-1, keepdims=True)
    return centred * lax.rsqrt(spread + EPSILON) * scales


def gelu(x):
    return 0.5 * x * (1.0 + jnp.tanh(x * (GELU_A + GELU_B * (x * x))))


def attend_tile(qkv, mix, row0, key_mask, value_mask, ones_block, score_mask):
    channels = mix.shape[-1]
    rows = pl.ds(row0, CELLS)
    for group in range(channels // GROUP):
        lanes = group * GROUP

        def part(index):
            return qkv[rows, index * channels + lanes : index * channels + lanes + GROUP]

        q_high, q_low = halves(part(0) * SCORE_SCALE)
        keys = part(1)
        k_high, k_low = halves(jnp.concatenate([keys, keys], axis=0).T)
        v_high, v_low = halves(part(2))

        def key_block(tile):
            return jnp.concatenate([tile] * (PACK // 2), axis=1) * key_mask[...]

        def value_block(tile):
            return jnp.concatenate([tile] * PACK, axis=0) * value_mask[...]

        k_high, k_low = key_block(k_high), key_block(k_low)
        left = jnp.concatenate([q_high, q_low, q_high], axis=1)
        scores = dot(left, jnp.concatenate([k_high, k_high, k_low], axis=0))
        weights = jnp.exp2(EXP_SCALE * jnp.tanh(scores))
        if score_mask is not None:
            weights = weights * score_mask[...]
        w_high, w_low = halves(weights)
        v_first = jnp.concatenate([value_block(v_high), ones_block], axis=1)
        v_all = jnp.concatenate(
            [
                v_first,
                v_first,
                jnp.concatenate([value_block(v_low), jnp.zeros_like(ones_block)], axis=1),
            ],
            axis=0,
        )
        summed = dot(jnp.concatenate([w_high, w_low, w_high], axis=1), v_all)
        mix[rows, lanes : lanes + GROUP] = summed[:, :GROUP] / summed[:, GROUP:]


def finish(stream, mixture, w_out, gain, w_up, w_down, chunk=512):
    stream = stream + dot3(mixture, *[w[...] for w in w_out])
    normed = layer_norm(stream, gain[...])
    n_high, n_low = halves(normed)
    left = jnp.concatenate([n_high, n_low, n_high], axis=1)
    up_high, up_low = w_up
    down_high, down_low = w_down
    total = stream
    for start in range(0, up_high.shape[1], chunk):
        cut = slice(start, start + chunk)
        right = jnp.concatenate([up_high[:, cut], up_high[:, cut], up_low[:, cut]], axis=0)
        hidden = gelu(dot(left, right))
        total = total + dot3(hidden, down_high[cut, :], down_low[cut, :])
    return total


class Weights:
    def __init__(self, sources, staged, buffers, semaphores):
        self.sources, self.staged, self.buffers = sources, staged, buffers
        self.copies = [
            pltpu.make_async_copy(source, stage, semaphores.at[i])
            for i, (source, stage) in enumerate(zip(sources, staged))
        ]
        self.pairs = [buffers[i : i + 2] for i in range(0, 8, 2)]

    def start(self):
        for copy in self.copies:
            copy.start()

    def split(self, first, last, block=64):
        for i in range(first, last):
            self.copies[i].wait()
            stage, (high, low) = self.staged[i], self.pairs[i]

            @pl.loop(0, stage.shape[0] // block)
            def _(step):
                rows = pl.ds(pl.multiple_of(step * block, block), block)
                high[rows, :], low[rows, :] = halves(stage[rows, :])


def iota(shape, dim):
    return lax.broadcasted_iota(jnp.int32, shape, dim)


def as_mask(condition, dtype=BF16):
    return jnp.where(condition, 1.0, 0.0).astype(dtype)


def block_masks(key_mask, value_mask):
    shape = (GROUP, PACK * CELLS)
    key_mask[...] = as_mask(iota(shape, 0) // HDIM == iota(shape, 1) // CELLS)
    shape = shape[::-1]
    block = iota(shape, 0) // CELLS == iota(shape, 1) // HDIM
    value_mask[...] = as_mask(block)
    return block


def spatial_kernel(plans, *refs):
    tile_count = 3 * sum(plans)
    tiles, refs = refs[:tile_count], refs[tile_count:]
    gain_attn, gain_mlp = refs[:2]
    sources, out = refs[2:6], refs[6]
    qkv, mix, key_mask, value_mask, ones = refs[7:12]
    weights = Weights(sources, refs[12:16], refs[16:24], refs[24])
    w_qkv, w_out, w_up, w_down = weights.pairs
    step = pl.program_id(0)
    cols, channels = tiles[0].shape[1], mix.shape[-1]
    lane_tiles = cols // WIN
    windows = lane_tiles + 1
    tokens = windows * CELLS

    @pl.when(step == 0)
    def _():
        weights.start()
        block = block_masks(key_mask, value_mask)
        key = iota((PACK * CELLS, GROUP), 0) % CELLS
        key_row, key_col = key // WIN, key % WIN
        row, row_last = lax.axis_index("row"), lax.axis_size("row") - 1
        col, col_last = lax.axis_index("col"), lax.axis_size("col") - 1
        col_ok = [
            key_col < jnp.where(col > 0, WIN, HALF),
            key_col >= 0,
            key_col >= jnp.where(col < col_last, 0, HALF),
        ]
        row_ok = [
            key_row >= 0,
            key_row >= jnp.where(row > 0, 0, HALF),
            key_row < jnp.where(row < row_last, WIN, HALF),
        ]
        for i in range(ones.shape[0]):
            for j in range(3):
                ones[i, j] = as_mask(block & row_ok[i] & col_ok[j])
        weights.split(0, 1)

    upper = iota((1, 1, WIN, channels), 2) >= HALF

    def run(tiles):
        bands = len(tiles) // 6
        for band in range(bands):
            parts = []
            for part in (2 * band, 2 * band + 1):
                body, left, right = [tiles[3 * part + i] for i in range(3)]
                parts.append(
                    jnp.concatenate(
                        [
                            left[...].reshape(HALF, 1, WIN, channels),
                            body[...].reshape(HALF, lane_tiles, WIN, channels),
                            right[...].reshape(HALF, 1, WIN, channels),
                        ],
                        axis=1,
                    )
                )
            wide = jnp.concatenate(parts, axis=0)
            wide = jnp.where(upper, wide[:, :windows], wide[:, 1:]).transpose(1, 0, 2, 3)
            normed = layer_norm(wide.reshape(tokens, channels), gain_attn[...])
            projected = dot3(normed, w_qkv[0][...], w_qkv[1][...])
            qkv[band * tokens : (band + 1) * tokens, :] = projected
        for band in range(bands):
            kind = 0 if bands == 1 else band + 1

            def window(j, carry, band=band, kind=kind):
                edge = jnp.where(j == 0, 0, jnp.where(j == windows - 1, 2, 1))
                row0 = pl.multiple_of(band * tokens + j * CELLS, CELLS)
                attend_tile(qkv, mix, row0, key_mask, value_mask, ones[kind, edge], None)
                return carry

            lax.fori_loop(0, windows, window, 0, unroll=3)

        @pl.when(step == 0)
        def _():
            weights.split(1, 4)

        if bands == 1:
            stream = jnp.concatenate([tiles[0][...], tiles[3][...]], axis=0)
            blended = mix[:tokens, :].reshape(windows, WIN, WIN, channels)
        else:
            stream = jnp.concatenate([tiles[3][...], tiles[6][...]], axis=0)
            first = mix[:tokens, :].reshape(windows, WIN, WIN, channels)
            second = mix[tokens:, :].reshape(windows, WIN, WIN, channels)
            blended = jnp.concatenate([first[:, HALF:], second[:, :HALF]], axis=1)
        blended = jnp.where(upper, blended[1:], blended[:lane_tiles])
        stream = stream.reshape(WIN, lane_tiles, WIN, channels).transpose(1, 0, 2, 3)
        result = finish(
            stream.reshape(WIN * cols, channels),
            blended.reshape(WIN * cols, channels),
            w_out,
            gain_mlp,
            w_up,
            w_down,
        )
        result = result.reshape(lane_tiles, WIN, WIN, channels).transpose(1, 0, 2, 3)
        out[...] = result.reshape(out.shape)

    if len(plans) == 1:
        run(tiles)
    else:
        at = 0
        for i, plan in enumerate(plans):
            mine = tiles[at : at + 3 * plan]
            at += 3 * plan

            @pl.when(step == i)
            def _(mine=mine):
                run(mine)


def temporal_kernel(x, gain_attn, gain_mlp, *refs):
    sources, out = refs[:4], refs[4]
    qkv, mix, key_mask, value_mask, causal = refs[5:10]
    weights = Weights(sources, refs[10:14], refs[14:22], refs[22])
    w_qkv, w_out, w_up, w_down = weights.pairs
    first = pl.program_id(0) == 0
    frames, cells, channels = x.shape
    groups = cells // WIN

    @pl.when(first)
    def _():
        weights.start()
        block_masks(key_mask, value_mask)
        query, key = iota(causal.shape, 0), iota(causal.shape, 1) % CELLS
        same = query % WIN == key % WIN
        causal[...] = as_mask(same & (key // WIN <= query // WIN), F32)
        weights.split(0, 1)

    stream = x[...].reshape(frames, groups, WIN, channels).transpose(1, 0, 2, 3)
    stream = stream.reshape(frames * cells, channels)
    normed = layer_norm(stream, gain_attn[...])
    qkv[...] = dot3(normed, w_qkv[0][...], w_qkv[1][...])

    def cell_group(j, carry):
        row0 = pl.multiple_of(j * CELLS, CELLS)
        attend_tile(qkv, mix, row0, key_mask, value_mask, value_mask[...], causal)
        return carry

    lax.fori_loop(0, groups, cell_group, 0, unroll=4)

    @pl.when(first)
    def _():
        weights.split(1, 4)

    result = finish(stream, mix[...], w_out, gain_mlp, w_up, w_down)
    result = result.reshape(groups, frames, WIN, channels).transpose(1, 0, 2, 3)
    out[...] = result.reshape(out.shape)


def scratch(tokens, last_mask, weights):
    channels = weights[1].shape[0]
    return [
        pltpu.VMEM((tokens, 3 * channels), F32),
        pltpu.VMEM((tokens, channels), F32),
        pltpu.VMEM((GROUP, PACK * CELLS), BF16),
        pltpu.VMEM((PACK * CELLS, GROUP), BF16),
        last_mask,
        *[pltpu.VMEM(w.shape, F32) for w in weights],
        *[pltpu.VMEM(w.shape, BF16) for w in weights for _ in range(2)],
        pltpu.SemaphoreType.DMA((4,)),
    ]


PARAMS = dict(vmem_limit_bytes=58 * 1024 * 1024)


def whole(array):
    return pl.BlockSpec(array.shape, lambda i: (0,) * array.ndim)


def cost(tokens, channels, hidden):
    flops = 2 * 3 * tokens * channels * (4 * channels + 2 * hidden)
    return pl.CostEstimate(
        flops=2 * flops, bytes_accessed=8 * tokens * channels, transcendentals=tokens * hidden
    )


def spatial_call(plans, steps, gains, weights):
    cols, channels = plans[0][0][0][0].shape[1:]
    hidden = weights[2].shape[1]
    in_specs, operands = [], []
    for plan in plans:
        for arrays, index in plan:
            for array in arrays:
                in_specs.append(
                    pl.BlockSpec((HALF,) + array.shape[1:], lambda i, index=index: (index(i), 0, 0))
                )
                operands.append(array)
    in_specs += [whole(gain) for gain in gains]
    in_specs += [pl.BlockSpec(memory_space=pl.ANY)] * 4
    bands = max(len(plan) for plan in plans) // 2
    ones = pltpu.VMEM((2 * bands - 1, 3, PACK * CELLS, GROUP), BF16)
    tokens = bands * WIN * (cols + WIN)
    return pl.pallas_call(
        functools.partial(spatial_kernel, [len(plan) for plan in plans]),
        grid=(steps,),
        in_specs=in_specs,
        out_specs=pl.BlockSpec((WIN, 1, cols, channels), lambda i: (0, i, 0, 0)),
        out_shape=jax.ShapeDtypeStruct((WIN, steps, cols, channels), F32),
        scratch_shapes=scratch(tokens, ones, weights),
        compiler_params=pltpu.CompilerParams(**PARAMS),
        cost_estimate=cost(steps * WIN * cols, channels, hidden),
        name="spatial",
    )(*operands, *gains, *weights)


def temporal_call(x, gains, weights, cells=64):
    frames, count, channels = x.shape
    hidden = weights[2].shape[1]
    block = pl.BlockSpec((frames, cells, channels), lambda i: (0, i, 0))
    causal = pltpu.VMEM((CELLS, PACK * CELLS), F32)
    return pl.pallas_call(
        temporal_kernel,
        grid=(count // cells,),
        in_specs=[block, *[whole(g) for g in gains]] + [pl.BlockSpec(memory_space=pl.ANY)] * 4,
        out_specs=block,
        out_shape=jax.ShapeDtypeStruct(x.shape, F32),
        scratch_shapes=scratch(frames * cells, causal, weights),
        compiler_params=pltpu.CompilerParams(**PARAMS),
        cost_estimate=cost(frames * count, channels, hidden),
        name="temporal",
    )(x, *gains, *weights)


def exchange(x):
    return lax.all_to_all(x, "tm", split_axis=0, concat_axis=0, tiled=True)


def neighbours(high_edge, low_edge, axis):
    count = lax.axis_size(axis)
    forward = [(i, i + 1) for i in range(count - 1)]
    backward = [(target, source) for source, target in forward]
    return lax.ppermute(high_edge, axis, forward), lax.ppermute(low_edge, axis, backward)


def per_device(
    tokens,
    spatial_norm,
    spatial_qkv,
    spatial_out,
    spatial_mlpnorm,
    spatial_up,
    spatial_down,
    temporal_norm,
    temporal_qkv,
    temporal_out,
    temporal_mlpnorm,
    temporal_up,
    temporal_down,
):
    _, row_n, col_n, channels = tokens.shape
    tokens = tokens.reshape(row_n, col_n, channels)
    left, right = neighbours(tokens[:, -WIN:], tokens[:, :WIN], "col")
    above, below = neighbours(tokens[-HALF:], tokens[:HALF], "row")
    far_left, far_right = neighbours(
        jnp.concatenate([above[:, -WIN:], below[:, -WIN:]], axis=0),
        jnp.concatenate([above[:, :WIN], below[:, :WIN]], axis=0),
        "col",
    )
    s_weights = (spatial_qkv, spatial_out, spatial_up, spatial_down)
    t_weights = (temporal_qkv, temporal_out, temporal_up, temporal_down)
    s_gains = (spatial_norm, spatial_mlpnorm)
    t_gains = (temporal_norm, temporal_mlpnorm)
    near = (tokens, left, right)
    last = row_n // HALF - 1
    inner = row_n // WIN - 1
    early = inner - 1

    def strip(first):
        return [(near, lambda i: 2 * (i + first) + 1), (near, lambda i: 2 * (i + first) + 2)]

    late = [(near, lambda i: 2 * early + 1), (near, lambda i: 2 * early + 2)]
    edge = [
        ((above, far_left[:HALF], far_right[:HALF]), lambda i: 0),
        (near, lambda i: 0),
        (near, lambda i: last),
        ((below, far_left[HALF:], far_right[HALF:]), lambda i: 0),
    ]
    pieces = [
        spatial_call([strip(0)], early, s_gains, s_weights),
        spatial_call([late, edge], 2, s_gains, s_weights),
    ]
    results = []
    for piece in pieces:
        arrived = exchange(piece.reshape(WIN, -1, channels))
        done = temporal_call(arrived, t_gains, t_weights)
        results.append(exchange(done).reshape(piece.shape))
    inner_rows = jnp.concatenate([results[0], results[1][:, :1]], axis=1).transpose(1, 0, 2, 3)
    inner_rows = inner_rows.reshape(-1, col_n, channels)
    edges = results[1][:, 1]
    outcome = jnp.concatenate([edges[:HALF], inner_rows, edges[HALF:]], axis=0)
    return outcome.reshape(1, row_n, col_n, channels)


def solution(mesh):
    placed = (P("tm", "row", "col", None),) + (P(),) * 12
    return jax.shard_map(
        per_device,
        mesh=mesh,
        in_specs=placed,
        out_specs=P("tm", "row", "col", None),
        check_vma=False,
    )
```

```python
import functools
import math

import jax
import jax.numpy as jnp
from jax import lax
from jax.experimental import pallas as pl
from jax.experimental.pallas import tpu as pltpu
from jax.sharding import PartitionSpec as P

HDIM = 32
WIN = 8
HALF = WIN // 2
EPSILON = 1e-05
SOFTCAP = 20.0
GROUP = 128
PACK = GROUP // HDIM
CELLS = WIN * WIN
SCORE_SCALE = 1.0 / (SOFTCAP * math.sqrt(HDIM))
EXP_SCALE = SOFTCAP * math.log2(math.e)
GELU_A = math.sqrt(2.0 / math.pi)
GELU_B = 0.044715 * GELU_A
BF16 = jnp.bfloat16
F32 = jnp.float32


def halves(value):
    high = value.astype(BF16)
    low = (value - high.astype(F32)).astype(BF16)
    return high, low


def dot(left, right, contract=((1,), (0,))):
    return lax.dot_general(left, right, (contract, ((), ())), preferred_element_type=F32)


def dot3(value, weight_high, weight_low):
    high, low = halves(value)
    left = jnp.concatenate([high, low, high], axis=1)
    right = jnp.concatenate([weight_high, weight_high, weight_low], axis=0)
    return dot(left, right)


def layer_norm(inputs, scales):
    average = jnp.mean(inputs, axis=-1, keepdims=True)
    centred = inputs - average
    spread = jnp.mean(centred * centred, axis=-1, keepdims=True)
    return centred * lax.rsqrt(spread + EPSILON) * scales


def gelu(x):
    return 0.5 * x * (1.0 + jnp.tanh(x * (GELU_A + GELU_B * (x * x))))


def swap(tile):
    return jnp.concatenate([tile[:, CELLS:], tile[:, :CELLS]], axis=1)


def attend_tile(qkv, mix, row0, key_mask, ones_block, score_mask):
    channels = mix.shape[-1]
    front = iota((CELLS, 2 * CELLS), 1) < CELLS
    heads = iota((CELLS, 2 * GROUP), 1) % GROUP // HDIM
    rows = pl.ds(row0, CELLS)
    for group in range(channels // GROUP):
        lanes = group * GROUP

        def part(index):
            return qkv[rows, index * channels + lanes : index * channels + lanes + GROUP]

        q_high, q_low = halves(part(0) * SCORE_SCALE)
        keys = part(1)
        k_high, k_low = halves(jnp.concatenate([keys, keys], axis=0).T)
        v_high, v_low = halves(part(2))

        def key_block(tile):
            return jnp.concatenate([tile] * (PACK // 2), axis=1) * key_mask[...]

        k_high, k_low = key_block(k_high), key_block(k_low)
        left = jnp.concatenate([q_high, q_low, q_high], axis=1)
        scores = dot(left, jnp.concatenate([k_high, k_high, k_low], axis=0))
        weights = jnp.exp2(EXP_SCALE * jnp.tanh(scores))
        if score_mask is not None:
            weights = weights * score_mask[...]
        w_high, w_low = halves(weights)
        stacked = []
        for pair in range(0, PACK, 2):
            cut = slice(pair * CELLS, (pair + 2) * CELLS)
            high, low = w_high[:, cut], w_low[:, cut]
            turned_low, turned_high = swap(low), swap(high)
            stacked.append(jnp.concatenate([jnp.where(front, high, turned_low), high], axis=1))
            stacked.append(jnp.concatenate([jnp.where(front, turned_low, high), turned_high], axis=1))
        v_all = jnp.concatenate(
            [
                jnp.concatenate([v_high, v_high, v_low, jnp.zeros_like(v_low)], axis=0),
                ones_block,
            ],
            axis=1,
        )
        summed = dot(jnp.concatenate(stacked, axis=0), v_all)
        total = summed[:CELLS]
        for head in range(1, PACK):
            total = jnp.where(heads == head, summed[head * CELLS : (head + 1) * CELLS], total)
        mix[rows, lanes : lanes + GROUP] = total[:, :GROUP] / total[:, GROUP:]


def finish(stream, mixture, w_out, gain, w_up, w_down, chunk=512):
    stream = stream + dot3(mixture, *[w[...] for w in w_out])
    normed = layer_norm(stream, gain[...])
    n_high, n_low = halves(normed)
    left = jnp.concatenate([n_high, n_low, n_high], axis=1)
    up_high, up_low = w_up
    down_high, down_low = w_down
    total = stream
    for start in range(0, up_high.shape[1], chunk):
        cut = slice(start, start + chunk)
        right = jnp.concatenate([up_high[:, cut], up_high[:, cut], up_low[:, cut]], axis=0)
        hidden = gelu(dot(left, right))
        total = total + dot3(hidden, down_high[cut, :], down_low[cut, :])
    return total


class Weights:
    def __init__(self, sources, staged, buffers, semaphores):
        self.sources, self.staged, self.buffers = sources, staged, buffers
        self.copies = [
            pltpu.make_async_copy(source, stage, semaphores.at[i])
            for i, (source, stage) in enumerate(zip(sources, staged))
        ]
        self.pairs = [buffers[i : i + 2] for i in range(0, 8, 2)]

    def start(self):
        for copy in self.copies:
            copy.start()

    def split(self, first, last, block=64):
        for i in range(first, last):
            self.copies[i].wait()
            stage, (high, low) = self.staged[i], self.pairs[i]

            @pl.loop(0, stage.shape[0] // block)
            def _(step):
                rows = pl.ds(pl.multiple_of(step * block, block), block)
                high[rows, :], low[rows, :] = halves(stage[rows, :])


def iota(shape, dim):
    return lax.broadcasted_iota(jnp.int32, shape, dim)


def as_mask(condition, dtype=BF16):
    return jnp.where(condition, 1.0, 0.0).astype(dtype)


def fill_key_mask(key_mask):
    shape = (GROUP, PACK * CELLS)
    key_mask[...] = as_mask(iota(shape, 0) // HDIM == iota(shape, 1) // CELLS)


def spatial_kernel(plans, after, *refs):
    tile_count = 3 * sum(plans)
    tiles, refs = refs[:tile_count], refs[tile_count:]
    gain_attn, gain_mlp = refs[:2]
    sources, refs = refs[2:6], refs[6 + after :]
    out, qkv, mix, key_mask, ones = refs[:5]
    weights = Weights(sources, refs[5:9], refs[9:17], refs[17])
    w_qkv, w_out, w_up, w_down = weights.pairs
    step = pl.program_id(0)
    cols, channels = tiles[0].shape[1], mix.shape[-1]
    lane_tiles = cols // WIN
    windows = lane_tiles + 1
    tokens = windows * CELLS

    @pl.when(step == 0)
    def _():
        weights.start()
        fill_key_mask(key_mask)
        position = iota((PACK * CELLS, GROUP), 0)
        key = position % CELLS
        key_row, key_col = key // WIN, key % WIN
        row, row_last = lax.axis_index("row"), lax.axis_size("row") - 1
        col, col_last = lax.axis_index("col"), lax.axis_size("col") - 1
        col_ok = [
            key_col < jnp.where(col > 0, WIN, HALF),
            key_col >= 0,
            key_col >= jnp.where(col < col_last, 0, HALF),
        ]
        row_ok = [
            key_row >= 0,
            key_row >= jnp.where(row > 0, 0, HALF),
            key_row < jnp.where(row < row_last, WIN, HALF),
        ]
        for i in range(ones.shape[0]):
            for j in range(3):
                ones[i, j] = as_mask((position < 2 * CELLS) & row_ok[i] & col_ok[j])
        weights.split(0, 1)

    upper = iota((1, 1, WIN, channels), 2) >= HALF

    def run(tiles):
        bands = len(tiles) // 6
        for band in range(bands):
            parts = []
            for part in (2 * band, 2 * band + 1):
                body, left, right = [tiles[3 * part + i] for i in range(3)]
                parts.append(
                    jnp.concatenate(
                        [
                            left[...].reshape(HALF, 1, WIN, channels),
                            body[...].reshape(HALF, lane_tiles, WIN, channels),
                            right[...].reshape(HALF, 1, WIN, channels),
                        ],
                        axis=1,
                    )
                )
            wide = jnp.concatenate(parts, axis=0)
            wide = jnp.where(upper, wide[:, :windows], wide[:, 1:]).transpose(1, 0, 2, 3)
            normed = layer_norm(wide.reshape(tokens, channels), gain_attn[...])
            projected = dot3(normed, w_qkv[0][...], w_qkv[1][...])
            qkv[band * tokens : (band + 1) * tokens, :] = projected
        for band in range(bands):
            kind = 0 if bands == 1 else band + 1

            def window(j, carry, band=band, kind=kind):
                edge = jnp.where(j == 0, 0, jnp.where(j == windows - 1, 2, 1))
                row0 = pl.multiple_of(band * tokens + j * CELLS, CELLS)
                attend_tile(qkv, mix, row0, key_mask, ones[kind, edge], None)
                return carry

            lax.fori_loop(0, windows, window, 0, unroll=3)

        @pl.when(step == 0)
        def _():
            weights.split(1, 4)

        if bands == 1:
            stream = jnp.concatenate([tiles[0][...], tiles[3][...]], axis=0)
            blended = mix[:tokens, :].reshape(windows, WIN, WIN, channels)
        else:
            stream = jnp.concatenate([tiles[3][...], tiles[6][...]], axis=0)
            first = mix[:tokens, :].reshape(windows, WIN, WIN, channels)
            second = mix[tokens:, :].reshape(windows, WIN, WIN, channels)
            blended = jnp.concatenate([first[:, HALF:], second[:, :HALF]], axis=1)
        blended = jnp.where(upper, blended[1:], blended[:lane_tiles])
        stream = stream.reshape(WIN, lane_tiles, WIN, channels).transpose(1, 0, 2, 3)
        result = finish(
            stream.reshape(WIN * cols, channels),
            blended.reshape(WIN * cols, channels),
            w_out,
            gain_mlp,
            w_up,
            w_down,
        )
        result = result.reshape(lane_tiles, WIN, WIN, channels).transpose(1, 0, 2, 3)
        out[...] = result.reshape(out.shape)

    if len(plans) == 1:
        run(tiles)
    else:
        at = 0
        for i, plan in enumerate(plans):
            mine = tiles[at : at + 3 * plan]
            at += 3 * plan

            @pl.when(step == i)
            def _(mine=mine):
                run(mine)


def temporal_kernel(after, x, gain_attn, gain_mlp, *refs):
    sources, refs = refs[:4], refs[4 + after :]
    out, qkv, mix, key_mask, causal = refs[:5]
    weights = Weights(sources, refs[5:9], refs[9:17], refs[17])
    w_qkv, w_out, w_up, w_down = weights.pairs
    first = pl.program_id(0) == 0
    frames, cells, channels = x.shape
    groups = cells // WIN

    @pl.when(first)
    def _():
        weights.start()
        fill_key_mask(key_mask)
        query, key = iota(causal.shape, 0), iota(causal.shape, 1) % CELLS
        same = query % WIN == key % WIN
        causal[...] = as_mask(same & (key // WIN <= query // WIN), F32)
        weights.split(0, 1)

    stream = x[...].reshape(frames, groups, WIN, channels).transpose(1, 0, 2, 3)
    stream = stream.reshape(frames * cells, channels)
    normed = layer_norm(stream, gain_attn[...])
    qkv[...] = dot3(normed, w_qkv[0][...], w_qkv[1][...])

    every = as_mask(iota((PACK * CELLS, GROUP), 0) < 2 * CELLS)

    def cell_group(j, carry):
        row0 = pl.multiple_of(j * CELLS, CELLS)
        attend_tile(qkv, mix, row0, key_mask, every, causal)
        return carry

    lax.fori_loop(0, groups, cell_group, 0, unroll=4)

    @pl.when(first)
    def _():
        weights.split(1, 4)

    result = finish(stream, mix[...], w_out, gain_mlp, w_up, w_down)
    result = result.reshape(groups, frames, WIN, channels).transpose(1, 0, 2, 3)
    out[...] = result.reshape(out.shape)


def scratch(tokens, last_mask, weights):
    channels = weights[1].shape[0]
    return [
        pltpu.VMEM((tokens, 3 * channels), F32),
        pltpu.VMEM((tokens, channels), F32),
        pltpu.VMEM((GROUP, PACK * CELLS), BF16),
        last_mask,
        *[pltpu.VMEM(w.shape, F32) for w in weights],
        *[pltpu.VMEM(w.shape, BF16) for w in weights for _ in range(2)],
        pltpu.SemaphoreType.DMA((4,)),
    ]


PARAMS = dict(vmem_limit_bytes=58 * 1024 * 1024)


def whole(array):
    return pl.BlockSpec(array.shape, lambda i: (0,) * array.ndim)


def cost(tokens, channels, hidden):
    flops = 2 * 3 * tokens * channels * (4 * channels + 2 * hidden)
    return pl.CostEstimate(
        flops=2 * flops, bytes_accessed=8 * tokens * channels, transcendentals=tokens * hidden
    )


def spatial_call(plans, steps, gains, weights, after=()):
    cols, channels = plans[0][0][0][0].shape[1:]
    hidden = weights[2].shape[1]
    in_specs, operands = [], []
    for plan in plans:
        for arrays, index in plan:
            for array in arrays:
                in_specs.append(
                    pl.BlockSpec((HALF,) + array.shape[1:], lambda i, index=index: (index(i), 0, 0))
                )
                operands.append(array)
    in_specs += [whole(gain) for gain in gains]
    in_specs += [pl.BlockSpec(memory_space=pl.ANY)] * (4 + len(after))
    bands = max(len(plan) for plan in plans) // 2
    ones = pltpu.VMEM((2 * bands - 1, 3, PACK * CELLS, GROUP), BF16)
    tokens = bands * WIN * (cols + WIN)
    return pl.pallas_call(
        functools.partial(spatial_kernel, [len(plan) for plan in plans], len(after)),
        grid=(steps,),
        in_specs=in_specs,
        out_specs=pl.BlockSpec((WIN, 1, cols, channels), lambda i: (0, i, 0, 0)),
        out_shape=jax.ShapeDtypeStruct((WIN, steps, cols, channels), F32),
        scratch_shapes=scratch(tokens, ones, weights),
        compiler_params=pltpu.CompilerParams(**PARAMS),
        cost_estimate=cost(steps * WIN * cols, channels, hidden),
        name="spatial",
    )(*operands, *gains, *weights, *after)


def temporal_call(x, gains, weights, after=(), cells=64):
    frames, count, channels = x.shape
    hidden = weights[2].shape[1]
    block = pl.BlockSpec((frames, cells, channels), lambda i: (0, i, 0))
    causal = pltpu.VMEM((CELLS, PACK * CELLS), F32)
    return pl.pallas_call(
        functools.partial(temporal_kernel, len(after)),
        grid=(count // cells,),
        in_specs=[block, *[whole(g) for g in gains]] + [pl.BlockSpec(memory_space=pl.ANY)] * (4 + len(after)),
        out_specs=block,
        out_shape=jax.ShapeDtypeStruct(x.shape, F32),
        scratch_shapes=scratch(frames * cells, causal, weights),
        compiler_params=pltpu.CompilerParams(**PARAMS),
        cost_estimate=cost(frames * count, channels, hidden),
        name="temporal",
    )(x, *gains, *weights, *after)


def exchange(x):
    return lax.all_to_all(x, "tm", split_axis=0, concat_axis=0, tiled=True)


def neighbours(high_edge, low_edge, axis):
    count = lax.axis_size(axis)
    forward = [(i, i + 1) for i in range(count - 1)]
    backward = [(target, source) for source, target in forward]
    return lax.ppermute(high_edge, axis, forward), lax.ppermute(low_edge, axis, backward)


def per_device(
    tokens,
    spatial_norm,
    spatial_qkv,
    spatial_out,
    spatial_mlpnorm,
    spatial_up,
    spatial_down,
    temporal_norm,
    temporal_qkv,
    temporal_out,
    temporal_mlpnorm,
    temporal_up,
    temporal_down,
):
    _, row_n, col_n, channels = tokens.shape
    tokens = tokens.reshape(row_n, col_n, channels)
    left, right = neighbours(tokens[:, -WIN:], tokens[:, :WIN], "col")
    above, below = neighbours(tokens[-HALF:], tokens[:HALF], "row")
    corners_above, corners_below = neighbours(
        jnp.concatenate([left[-HALF:], right[-HALF:]], axis=0),
        jnp.concatenate([left[:HALF], right[:HALF]], axis=0),
        "row",
    )
    s_weights = (spatial_qkv, spatial_out, spatial_up, spatial_down)
    t_weights = (temporal_qkv, temporal_out, temporal_up, temporal_down)
    s_gains = (spatial_norm, spatial_mlpnorm)
    t_gains = (temporal_norm, temporal_mlpnorm)
    near = (tokens, left, right)
    last = row_n // HALF - 1
    inner = row_n // WIN - 1
    early = inner - 1

    def strip(first):
        return [(near, lambda i: 2 * (i + first) + 1), (near, lambda i: 2 * (i + first) + 2)]

    late = [(near, lambda i: 2 * early + 1), (near, lambda i: 2 * early + 2)]
    edge = [
        ((above, corners_above[:HALF], corners_above[HALF:]), lambda i: 0),
        (near, lambda i: 0),
        (near, lambda i: last),
        ((below, corners_below[:HALF], corners_below[HALF:]), lambda i: 0),
    ]
    early_piece = spatial_call([strip(0)], early, s_gains, s_weights)
    late_piece = spatial_call([late, edge], 2, s_gains, s_weights, (early_piece,))
    results, before = [], ()
    for piece in (early_piece, late_piece):
        arrived = exchange(piece.reshape(WIN, -1, channels))
        done = temporal_call(arrived, t_gains, t_weights, before)
        before = (done,)
        results.append(exchange(done).reshape(piece.shape))
    inner_rows = results[0].transpose(1, 0, 2, 3).reshape(-1, col_n, channels)
    strip_rows, edges = results[1][:, 0], results[1][:, 1]
    outcome = jnp.pad(inner_rows, ((HALF, row_n - HALF - inner_rows.shape[0]), (0, 0), (0, 0)))
    outcome = lax.dynamic_update_slice(outcome, strip_rows, (HALF + early * WIN, 0, 0))
    outcome = lax.dynamic_update_slice(outcome, edges[:HALF], (0, 0, 0))
    outcome = lax.dynamic_update_slice(outcome, edges[HALF:], (row_n - HALF, 0, 0))
    return outcome.reshape(1, row_n, col_n, channels)


def solution(mesh):
    placed = (P("tm", "row", "col", None),) + (P(),) * 12
    return jax.shard_map(
        per_device,
        mesh=mesh,
        in_specs=placed,
        out_specs=P("tm", "row", "col", None),
        check_vma=False,
    )
```

```python
import functools
import math

import jax
import jax.numpy as jnp
from jax import lax
from jax.experimental import pallas as pl
from jax.experimental.pallas import tpu as pltpu
from jax.sharding import PartitionSpec as P

HDIM = 32
WIN = 8
HALF = WIN // 2
EPSILON = 1e-05
SOFTCAP = 20.0
GROUP = 128
PACK = GROUP // HDIM
CELLS = WIN * WIN
SCORE_SCALE = 1.0 / (SOFTCAP * math.sqrt(HDIM))
EXP_SCALE = SOFTCAP * math.log2(math.e)
GELU_A = math.sqrt(2.0 / math.pi)
GELU_B = 0.044715 * GELU_A
BF16 = jnp.bfloat16
F32 = jnp.float32


def halves(value):
    high = value.astype(BF16)
    low = (value - high.astype(F32)).astype(BF16)
    return high, low


def dot(left, right, contract=((1,), (0,))):
    return lax.dot_general(left, right, (contract, ((), ())), preferred_element_type=F32)


def dot3(value, weight_high, weight_low):
    high, low = halves(value)
    left = jnp.concatenate([high, low, high], axis=1)
    right = jnp.concatenate([weight_high, weight_high, weight_low], axis=0)
    return dot(left, right)


def layer_norm(inputs, scales):
    average = jnp.mean(inputs, axis=-1, keepdims=True)
    centred = inputs - average
    spread = jnp.mean(centred * centred, axis=-1, keepdims=True)
    return centred * lax.rsqrt(spread + EPSILON) * scales


def gelu(x):
    return 0.5 * x * (1.0 + jnp.tanh(x * (GELU_A + GELU_B * (x * x))))


def fold(stacked):
    return stacked[:CELLS] + stacked[CELLS:]


def attend_tile(qkv, mix, row0, key_mask, value_mask, ones_block, score_mask):
    channels = mix.shape[-1]
    rows = pl.ds(row0, CELLS)
    for group in range(channels // GROUP):
        lanes = group * GROUP

        def part(index):
            return qkv[rows, index * channels + lanes : index * channels + lanes + GROUP]

        q_high, q_low = halves(part(0) * SCORE_SCALE)
        keys = part(1)
        k_high, k_low = halves(jnp.concatenate([keys, keys], axis=0).T)
        v_high, v_low = halves(part(2))

        def key_block(tile):
            return jnp.concatenate([tile] * (PACK // 2), axis=1) * key_mask[...]

        def value_block(tile):
            return jnp.concatenate([tile] * PACK, axis=0) * value_mask[...]

        left = jnp.concatenate([q_high, q_low], axis=0)
        right = jnp.concatenate([key_block(k_high), key_block(k_low)], axis=1)
        scores = fold(dot(left, right))
        scores = scores[:, : PACK * CELLS] + scores[:, PACK * CELLS :]
        weights = jnp.exp2(EXP_SCALE * jnp.tanh(scores))
        if score_mask is not None:
            weights = weights * score_mask[...]
        left = jnp.concatenate(halves(weights), axis=0)
        right = jnp.concatenate([value_block(v_high), ones_block, value_block(v_low)], axis=1)
        summed = fold(dot(left, right))
        total = summed[:, :GROUP] + summed[:, 2 * GROUP :]
        mix[rows, lanes : lanes + GROUP] = total / summed[:, GROUP : 2 * GROUP]


def finish(stream, mixture, w_out, gain, w_up, w_down, chunk=512):
    stream = stream + dot3(mixture, *[w[...] for w in w_out])
    normed = layer_norm(stream, gain[...])
    n_high, n_low = halves(normed)
    left = jnp.concatenate([n_high, n_low, n_high], axis=1)
    up_high, up_low = w_up
    down_high, down_low = w_down
    total = stream
    for start in range(0, up_high.shape[1], chunk):
        cut = slice(start, start + chunk)
        right = jnp.concatenate([up_high[:, cut], up_high[:, cut], up_low[:, cut]], axis=0)
        hidden = gelu(dot(left, right))
        total = total + dot3(hidden, down_high[cut, :], down_low[cut, :])
    return total


class Weights:
    def __init__(self, sources, staged, buffers, semaphores):
        self.sources, self.staged, self.buffers = sources, staged, buffers
        self.copies = [
            pltpu.make_async_copy(source, stage, semaphores.at[i])
            for i, (source, stage) in enumerate(zip(sources, staged))
        ]
        self.pairs = [buffers[i : i + 2] for i in range(0, 8, 2)]

    def start(self):
        for copy in self.copies:
            copy.start()

    def split(self, first, last, block=64):
        for i in range(first, last):
            self.copies[i].wait()
            stage, (high, low) = self.staged[i], self.pairs[i]

            @pl.loop(0, stage.shape[0] // block)
            def _(step):
                rows = pl.ds(pl.multiple_of(step * block, block), block)
                high[rows, :], low[rows, :] = halves(stage[rows, :])


def iota(shape, dim):
    return lax.broadcasted_iota(jnp.int32, shape, dim)


def as_mask(condition, dtype=BF16):
    return jnp.where(condition, 1.0, 0.0).astype(dtype)


def block_masks(key_mask, value_mask):
    shape = (GROUP, PACK * CELLS)
    key_mask[...] = as_mask(iota(shape, 0) // HDIM == iota(shape, 1) // CELLS)
    shape = shape[::-1]
    block = iota(shape, 0) // CELLS == iota(shape, 1) // HDIM
    value_mask[...] = as_mask(block)
    return block


def spatial_kernel(plans, after, *refs):
    tile_count = sum(sum(plan) for plan in plans)
    tiles, refs = refs[:tile_count], refs[tile_count:]
    gain_attn, gain_mlp = refs[:2]
    sources, refs = refs[2:6], refs[6 + after :]
    out, qkv, mix, key_mask, value_mask, ones = refs[:6]
    weights = Weights(sources, refs[6:10], refs[10:18], refs[18])
    w_qkv, w_out, w_up, w_down = weights.pairs
    step = pl.program_id(0)
    cols, channels = out.shape[2], mix.shape[-1]
    lane_tiles = cols // WIN
    windows = lane_tiles + 1
    tokens = windows * CELLS

    @pl.when(step == 0)
    def _():
        weights.start()
        block = block_masks(key_mask, value_mask)
        key = iota((PACK * CELLS, GROUP), 0) % CELLS
        key_row, key_col = key // WIN, key % WIN
        row, row_last = lax.axis_index("row"), lax.axis_size("row") - 1
        col, col_last = lax.axis_index("col"), lax.axis_size("col") - 1
        col_ok = [
            key_col < jnp.where(col > 0, WIN, HALF),
            key_col >= 0,
            key_col >= jnp.where(col < col_last, 0, HALF),
        ]
        row_ok = [
            key_row >= 0,
            key_row >= jnp.where(row > 0, 0, HALF),
            key_row < jnp.where(row < row_last, WIN, HALF),
        ]
        for i in range(ones.shape[0]):
            for j in range(3):
                ones[i, j] = as_mask(block & row_ok[i] & col_ok[j])
        weights.split(0, 1)

    upper = iota((1, 1, WIN, channels), 2) >= HALF

    def run(pieces):
        bands = len(pieces) // 2
        for band in range(bands):
            parts = []
            for piece in pieces[2 * band : 2 * band + 2]:
                parts.append(
                    jnp.concatenate([t[...].reshape(HALF, -1, WIN, channels) for t in piece], axis=1)
                )
            wide = jnp.concatenate(parts, axis=0)
            wide = jnp.where(upper, wide[:, :windows], wide[:, 1:]).transpose(1, 0, 2, 3)
            normed = layer_norm(wide.reshape(tokens, channels), gain_attn[...])
            projected = dot3(normed, w_qkv[0][...], w_qkv[1][...])
            qkv[band * tokens : (band + 1) * tokens, :] = projected
        for band in range(bands):
            kind = 0 if bands == 1 else band + 1

            def window(j, carry, band=band, kind=kind):
                edge = jnp.where(j == 0, 0, jnp.where(j == windows - 1, 2, 1))
                row0 = pl.multiple_of(band * tokens + j * CELLS, CELLS)
                attend_tile(qkv, mix, row0, key_mask, value_mask, ones[kind, edge], None)
                return carry

            lax.fori_loop(0, windows, window, 0, unroll=3)

        @pl.when(step == 0)
        def _():
            weights.split(1, 4)

        if bands == 1:
            stream = jnp.concatenate([piece[1][...] for piece in pieces], axis=0)
            blended = mix[:tokens, :].reshape(windows, WIN, WIN, channels)
        else:
            stream = jnp.concatenate([piece[1][...] for piece in pieces[1:3]], axis=0)
            first = mix[:tokens, :].reshape(windows, WIN, WIN, channels)
            second = mix[tokens:, :].reshape(windows, WIN, WIN, channels)
            blended = jnp.concatenate([first[:, HALF:], second[:, :HALF]], axis=1)
        blended = jnp.where(upper, blended[1:], blended[:lane_tiles])
        stream = stream.reshape(WIN, lane_tiles, WIN, channels).transpose(1, 0, 2, 3)
        result = finish(
            stream.reshape(WIN * cols, channels),
            blended.reshape(WIN * cols, channels),
            w_out,
            gain_mlp,
            w_up,
            w_down,
        )
        result = result.reshape(lane_tiles, WIN, WIN, channels).transpose(1, 0, 2, 3)
        out[...] = result.reshape(out.shape)

    at = 0
    for i, plan in enumerate(plans):
        pieces = []
        for count in plan:
            pieces.append(tiles[at : at + count])
            at += count
        if len(plans) == 1:
            run(pieces)
        else:
            pl.when(step == i)(functools.partial(run, pieces))


def temporal_kernel(after, x, gain_attn, gain_mlp, *refs):
    sources, refs = refs[:4], refs[4 + after :]
    out, qkv, mix, key_mask, value_mask, causal = refs[:6]
    weights = Weights(sources, refs[6:10], refs[10:18], refs[18])
    w_qkv, w_out, w_up, w_down = weights.pairs
    first = pl.program_id(0) == 0
    frames, cells, channels = x.shape
    groups = cells // WIN

    @pl.when(first)
    def _():
        weights.start()
        block_masks(key_mask, value_mask)
        query, key = iota(causal.shape, 0), iota(causal.shape, 1) % CELLS
        same = query % WIN == key % WIN
        causal[...] = as_mask(same & (key // WIN <= query // WIN), F32)
        weights.split(0, 1)

    stream = x[...].reshape(frames, groups, WIN, channels).transpose(1, 0, 2, 3)
    stream = stream.reshape(frames * cells, channels)
    normed = layer_norm(stream, gain_attn[...])
    qkv[...] = dot3(normed, w_qkv[0][...], w_qkv[1][...])

    def cell_group(j, carry):
        row0 = pl.multiple_of(j * CELLS, CELLS)
        attend_tile(qkv, mix, row0, key_mask, value_mask, value_mask[...], causal)
        return carry

    lax.fori_loop(0, groups, cell_group, 0, unroll=4)

    @pl.when(first)
    def _():
        weights.split(1, 4)

    result = finish(stream, mix[...], w_out, gain_mlp, w_up, w_down)
    result = result.reshape(groups, frames, WIN, channels).transpose(1, 0, 2, 3)
    out[...] = result.reshape(out.shape)


def scratch(tokens, last_mask, weights):
    channels = weights[1].shape[0]
    return [
        pltpu.VMEM((tokens, 3 * channels), F32),
        pltpu.VMEM((tokens, channels), F32),
        pltpu.VMEM((GROUP, PACK * CELLS), BF16),
        pltpu.VMEM((PACK * CELLS, GROUP), BF16),
        last_mask,
        *[pltpu.VMEM(w.shape, F32) for w in weights],
        *[pltpu.VMEM(w.shape, BF16) for w in weights for _ in range(2)],
        pltpu.SemaphoreType.DMA((4,)),
    ]


PARAMS = dict(vmem_limit_bytes=58 * 1024 * 1024)


def whole(array):
    return pl.BlockSpec(array.shape, lambda i: (0,) * array.ndim)


def cost(tokens, channels, hidden):
    flops = 2 * 3 * tokens * channels * (4 * channels + 2 * hidden)
    return pl.CostEstimate(
        flops=2 * flops, bytes_accessed=8 * tokens * channels, transcendentals=tokens * hidden
    )


def spatial_call(plans, steps, gains, weights, after=()):
    cols, channels = plans[0][0][0][1].shape[1:]
    counts = [[len(arrays) for arrays, _ in plan] for plan in plans]
    hidden = weights[2].shape[1]
    in_specs, operands = [], []
    for plan in plans:
        for arrays, index in plan:
            for array in arrays:
                in_specs.append(
                    pl.BlockSpec((HALF,) + array.shape[1:], lambda i, index=index: (index(i), 0, 0))
                )
                operands.append(array)
    in_specs += [whole(gain) for gain in gains]
    in_specs += [pl.BlockSpec(memory_space=pl.ANY)] * (4 + len(after))
    bands = max(len(plan) for plan in plans) // 2
    ones = pltpu.VMEM((2 * bands - 1, 3, PACK * CELLS, GROUP), BF16)
    tokens = bands * WIN * (cols + WIN)
    return pl.pallas_call(
        functools.partial(spatial_kernel, counts, len(after)),
        grid=(steps,),
        in_specs=in_specs,
        out_specs=pl.BlockSpec((WIN, 1, cols, channels), lambda i: (0, i, 0, 0)),
        out_shape=jax.ShapeDtypeStruct((WIN, steps, cols, channels), F32),
        scratch_shapes=scratch(tokens, ones, weights),
        compiler_params=pltpu.CompilerParams(**PARAMS),
        cost_estimate=cost(steps * WIN * cols, channels, hidden),
        name="spatial",
    )(*operands, *gains, *weights, *after)


def temporal_call(x, gains, weights, after=(), cells=64):
    frames, count, channels = x.shape
    hidden = weights[2].shape[1]
    block = pl.BlockSpec((frames, cells, channels), lambda i: (0, i, 0))
    causal = pltpu.VMEM((CELLS, PACK * CELLS), F32)
    return pl.pallas_call(
        functools.partial(temporal_kernel, len(after)),
        grid=(count // cells,),
        in_specs=[block, *[whole(g) for g in gains]] + [pl.BlockSpec(memory_space=pl.ANY)] * (4 + len(after)),
        out_specs=block,
        out_shape=jax.ShapeDtypeStruct(x.shape, F32),
        scratch_shapes=scratch(frames * cells, causal, weights),
        compiler_params=pltpu.CompilerParams(**PARAMS),
        cost_estimate=cost(frames * count, channels, hidden),
        name="temporal",
    )(x, *gains, *weights, *after)


def exchange(x):
    return lax.all_to_all(x, "tm", split_axis=0, concat_axis=0, tiled=True)


def neighbours(high_edge, low_edge, axis):
    count = lax.axis_size(axis)
    forward = [(i, i + 1) for i in range(count - 1)]
    backward = [(target, source) for source, target in forward]
    return lax.ppermute(high_edge, axis, forward), lax.ppermute(low_edge, axis, backward)


def per_device(
    tokens,
    spatial_norm,
    spatial_qkv,
    spatial_out,
    spatial_mlpnorm,
    spatial_up,
    spatial_down,
    temporal_norm,
    temporal_qkv,
    temporal_out,
    temporal_mlpnorm,
    temporal_up,
    temporal_down,
):
    _, row_n, col_n, channels = tokens.shape
    tokens = tokens.reshape(row_n, col_n, channels)
    left, right = neighbours(tokens[:, -WIN:], tokens[:, :WIN], "col")
    def widened(cut):
        return jnp.concatenate([left[cut], tokens[cut], right[cut]], axis=1)

    above, below = neighbours(widened(slice(-HALF, None)), widened(slice(HALF)), "row")
    s_weights = (spatial_qkv, spatial_out, spatial_up, spatial_down)
    t_weights = (temporal_qkv, temporal_out, temporal_up, temporal_down)
    s_gains = (spatial_norm, spatial_mlpnorm)
    t_gains = (temporal_norm, temporal_mlpnorm)
    near = (left, tokens, right)
    last = row_n // HALF - 1
    inner = row_n // WIN - 1
    early = inner - 1

    def strip(first):
        return [(near, lambda i: 2 * (i + first) + 1), (near, lambda i: 2 * (i + first) + 2)]

    late = [(near, lambda i: 2 * early + 1), (near, lambda i: 2 * early + 2)]
    edge = [
        ((above,), lambda i: 0),
        (near, lambda i: 0),
        (near, lambda i: last),
        ((below,), lambda i: 0),
    ]
    early_piece = spatial_call([strip(0)], early, s_gains, s_weights)
    late_piece = spatial_call([late, edge], 2, s_gains, s_weights, (early_piece,))
    results, before = [], ()
    for piece in (early_piece, late_piece):
        arrived = exchange(piece.reshape(WIN, -1, channels))
        done = temporal_call(arrived, t_gains, t_weights, before)
        before = (done,)
        results.append(exchange(done).reshape(piece.shape))
    inner_rows = results[0].transpose(1, 0, 2, 3).reshape(-1, col_n, channels)
    strip_rows, edges = results[1][:, 0], results[1][:, 1]
    outcome = jnp.pad(inner_rows, ((HALF, row_n - HALF - inner_rows.shape[0]), (0, 0), (0, 0)))
    outcome = lax.dynamic_update_slice(outcome, strip_rows, (HALF + early * WIN, 0, 0))
    outcome = lax.dynamic_update_slice(outcome, edges[:HALF], (0, 0, 0))
    outcome = lax.dynamic_update_slice(outcome, edges[HALF:], (row_n - HALF, 0, 0))
    return outcome.reshape(1, row_n, col_n, channels)


def solution(mesh):
    placed = (P("tm", "row", "col", None),) + (P(),) * 12
    return jax.shard_map(
        per_device,
        mesh=mesh,
        in_specs=placed,
        out_specs=P("tm", "row", "col", None),
        check_vma=False,
    )
```

```python
import functools
import math

import jax
import jax.numpy as jnp
from jax import lax
from jax.experimental import pallas as pl
from jax.experimental.pallas import tpu as pltpu
from jax.sharding import PartitionSpec as P

HDIM = 32
WIN = 8
HALF = WIN // 2
EPSILON = 1e-05
SOFTCAP = 20.0
GROUP = 128
PACK = GROUP // HDIM
CELLS = WIN * WIN
SCORE_SCALE = 1.0 / (SOFTCAP * math.sqrt(HDIM))
EXP_SCALE = SOFTCAP * math.log2(math.e)
GELU_A = math.sqrt(2.0 / math.pi)
GELU_B = 0.044715 * GELU_A
BF16 = jnp.bfloat16
F32 = jnp.float32


def halves(value):
    high = value.astype(BF16)
    low = (value - high.astype(F32)).astype(BF16)
    return high, low


def dot(left, right, contract=((1,), (0,))):
    return lax.dot_general(left, right, (contract, ((), ())), preferred_element_type=F32)


def dot3(value, weight_high, weight_low):
    high, low = halves(value)
    left = jnp.concatenate([high, low, high], axis=1)
    right = jnp.concatenate([weight_high, weight_high, weight_low], axis=0)
    return dot(left, right)


def layer_norm(inputs, scales):
    average = jnp.mean(inputs, axis=-1, keepdims=True)
    centred = inputs - average
    spread = jnp.mean(centred * centred, axis=-1, keepdims=True)
    return centred * lax.rsqrt(spread + EPSILON) * scales


def gelu(x):
    return 0.5 * x * (1.0 + jnp.tanh(x * (GELU_A + GELU_B * (x * x))))


def fold(stacked):
    return stacked[:CELLS] + stacked[CELLS:]


def attend_tile(qkv, mix, row0, key_mask, value_mask, ones_block, score_mask):
    channels = mix.shape[-1]
    rows = pl.ds(row0, CELLS)
    for group in range(channels // GROUP):
        lanes = group * GROUP

        def part(index):
            return qkv[rows, index * channels + lanes : index * channels + lanes + GROUP]

        q_high, q_low = halves(part(0) * SCORE_SCALE)
        keys = part(1)
        k_high, k_low = halves(jnp.concatenate([keys, keys], axis=0).T)
        v_high, v_low = halves(part(2))

        def key_block(tile):
            return jnp.concatenate([tile] * (PACK // 2), axis=1) * key_mask[...]

        def value_block(tile):
            return jnp.concatenate([tile] * PACK, axis=0) * value_mask[...]

        left = jnp.concatenate([q_high, q_low], axis=0)
        right = jnp.concatenate([key_block(k_high), key_block(k_low)], axis=1)
        scores = fold(dot(left, right))
        scores = scores[:, : PACK * CELLS] + scores[:, PACK * CELLS :]
        weights = jnp.exp2(EXP_SCALE * jnp.tanh(scores))
        if score_mask is not None:
            weights = weights * score_mask[...]
        left = jnp.concatenate(halves(weights), axis=0)
        right = jnp.concatenate([value_block(v_high), ones_block, value_block(v_low)], axis=1)
        summed = fold(dot(left, right))
        total = summed[:, :GROUP] + summed[:, 2 * GROUP :]
        mix[rows, lanes : lanes + GROUP] = total / summed[:, GROUP : 2 * GROUP]


def finish(stream, mixture, w_out, gain, w_up, w_down, chunk=512):
    stream = stream + dot3(mixture, *[w[...] for w in w_out])
    normed = layer_norm(stream, gain[...])
    n_high, n_low = halves(normed)
    left = jnp.concatenate([n_high, n_low, n_high], axis=1)
    up_high, up_low = w_up
    down_high, down_low = w_down
    total = stream
    for start in range(0, up_high.shape[1], chunk):
        cut = slice(start, start + chunk)
        right = jnp.concatenate([up_high[:, cut], up_high[:, cut], up_low[:, cut]], axis=0)
        hidden = gelu(dot(left, right))
        total = total + dot3(hidden, down_high[cut, :], down_low[cut, :])
    return total


class Weights:
    def __init__(self, sources, staged, buffers, semaphores):
        self.sources, self.staged, self.buffers = sources, staged, buffers
        self.copies = [
            pltpu.make_async_copy(source, stage, semaphores.at[i])
            for i, (source, stage) in enumerate(zip(sources, staged))
        ]
        self.pairs = [buffers[i : i + 2] for i in range(0, 8, 2)]

    def start(self):
        for copy in self.copies:
            copy.start()

    def split(self, first, last, block=64):
        for i in range(first, last):
            self.copies[i].wait()
            stage, (high, low) = self.staged[i], self.pairs[i]

            @pl.loop(0, stage.shape[0] // block)
            def _(step):
                rows = pl.ds(pl.multiple_of(step * block, block), block)
                high[rows, :], low[rows, :] = halves(stage[rows, :])


def iota(shape, dim):
    return lax.broadcasted_iota(jnp.int32, shape, dim)


def as_mask(condition, dtype=BF16):
    return jnp.where(condition, 1.0, 0.0).astype(dtype)


def block_masks(key_mask, value_mask):
    shape = (GROUP, PACK * CELLS)
    key_mask[...] = as_mask(iota(shape, 0) // HDIM == iota(shape, 1) // CELLS)
    shape = shape[::-1]
    block = iota(shape, 0) // CELLS == iota(shape, 1) // HDIM
    value_mask[...] = as_mask(block)
    return block


def spatial_kernel(plans, after, *refs):
    tile_count = sum(sum(plan) for plan in plans)
    tiles, refs = refs[:tile_count], refs[tile_count:]
    gain_attn, gain_mlp = refs[:2]
    sources, refs = refs[2:6], refs[6 + after :]
    out, qkv, mix, key_mask, value_mask, ones = refs[:6]
    weights = Weights(sources, refs[6:10], refs[10:18], refs[18])
    w_qkv, w_out, w_up, w_down = weights.pairs
    step = pl.program_id(0)
    cols, channels = out.shape[2], mix.shape[-1]
    lane_tiles = cols // WIN
    windows = lane_tiles + 1
    tokens = windows * CELLS

    @pl.when(step == 0)
    def _():
        weights.start()
        block = block_masks(key_mask, value_mask)
        key = iota((PACK * CELLS, GROUP), 0) % CELLS
        key_row, key_col = key // WIN, key % WIN
        row, row_last = lax.axis_index("row"), lax.axis_size("row") - 1
        col, col_last = lax.axis_index("col"), lax.axis_size("col") - 1
        col_ok = [
            key_col < jnp.where(col > 0, WIN, HALF),
            key_col >= 0,
            key_col >= jnp.where(col < col_last, 0, HALF),
        ]
        row_ok = [
            key_row >= 0,
            key_row >= jnp.where(row > 0, 0, HALF),
            key_row < jnp.where(row < row_last, WIN, HALF),
        ]
        for i in range(ones.shape[0]):
            for j in range(3):
                ones[i, j] = as_mask(block & row_ok[i] & col_ok[j])
        weights.split(0, 1)

    upper = iota((1, 1, WIN, channels), 2) >= HALF

    def run(pieces):
        bands = len(pieces) // 2
        for band in range(bands):
            parts = []
            for piece in pieces[2 * band : 2 * band + 2]:
                parts.append(
                    jnp.concatenate([t[...].reshape(HALF, -1, WIN, channels) for t in piece], axis=1)
                )
            wide = jnp.concatenate(parts, axis=0)
            wide = jnp.where(upper, wide[:, :windows], wide[:, 1:]).transpose(1, 0, 2, 3)
            normed = layer_norm(wide.reshape(tokens, channels), gain_attn[...])
            projected = dot3(normed, w_qkv[0][...], w_qkv[1][...])
            qkv[band * tokens : (band + 1) * tokens, :] = projected
        for band in range(bands):
            kind = 0 if bands == 1 else band + 1

            def window(j, carry, band=band, kind=kind):
                edge = jnp.where(j == 0, 0, jnp.where(j == windows - 1, 2, 1))
                row0 = pl.multiple_of(band * tokens + j * CELLS, CELLS)
                attend_tile(qkv, mix, row0, key_mask, value_mask, ones[kind, edge], None)
                return carry

            lax.fori_loop(0, windows, window, 0, unroll=9)

        @pl.when(step == 0)
        def _():
            weights.split(1, 4)

        if bands == 1:
            stream = jnp.concatenate([piece[1][...] for piece in pieces], axis=0)
            blended = mix[:tokens, :].reshape(windows, WIN, WIN, channels)
        else:
            stream = jnp.concatenate([piece[1][...] for piece in pieces[1:3]], axis=0)
            first = mix[:tokens, :].reshape(windows, WIN, WIN, channels)
            second = mix[tokens:, :].reshape(windows, WIN, WIN, channels)
            blended = jnp.concatenate([first[:, HALF:], second[:, :HALF]], axis=1)
        blended = jnp.where(upper, blended[1:], blended[:lane_tiles])
        stream = stream.reshape(WIN, lane_tiles, WIN, channels).transpose(1, 0, 2, 3)
        result = finish(
            stream.reshape(WIN * cols, channels),
            blended.reshape(WIN * cols, channels),
            w_out,
            gain_mlp,
            w_up,
            w_down,
        )
        result = result.reshape(lane_tiles, WIN, WIN, channels).transpose(1, 0, 2, 3)
        out[...] = result.reshape(out.shape)

    at = 0
    for i, plan in enumerate(plans):
        pieces = []
        for count in plan:
            pieces.append(tiles[at : at + count])
            at += count
        if len(plans) == 1:
            run(pieces)
        else:
            pl.when(step == i)(functools.partial(run, pieces))


def temporal_kernel(after, x, gain_attn, gain_mlp, *refs):
    sources, refs = refs[:4], refs[4 + after :]
    out, qkv, mix, key_mask, value_mask, causal = refs[:6]
    weights = Weights(sources, refs[6:10], refs[10:18], refs[18])
    w_qkv, w_out, w_up, w_down = weights.pairs
    first = pl.program_id(0) == 0
    frames, cells, channels = x.shape
    groups = cells // WIN

    @pl.when(first)
    def _():
        weights.start()
        block_masks(key_mask, value_mask)
        query, key = iota(causal.shape, 0), iota(causal.shape, 1) % CELLS
        same = query % WIN == key % WIN
        causal[...] = as_mask(same & (key // WIN <= query // WIN), F32)
        weights.split(0, 1)

    stream = x[...].reshape(frames, groups, WIN, channels).transpose(1, 0, 2, 3)
    stream = stream.reshape(frames * cells, channels)
    normed = layer_norm(stream, gain_attn[...])
    qkv[...] = dot3(normed, w_qkv[0][...], w_qkv[1][...])

    def cell_group(j, carry):
        row0 = pl.multiple_of(j * CELLS, CELLS)
        attend_tile(qkv, mix, row0, key_mask, value_mask, value_mask[...], causal)
        return carry

    lax.fori_loop(0, groups, cell_group, 0, unroll=8)

    @pl.when(first)
    def _():
        weights.split(1, 4)

    result = finish(stream, mix[...], w_out, gain_mlp, w_up, w_down)
    result = result.reshape(groups, frames, WIN, channels).transpose(1, 0, 2, 3)
    out[...] = result.reshape(out.shape)


def scratch(tokens, last_mask, weights):
    channels = weights[1].shape[0]
    return [
        pltpu.VMEM((tokens, 3 * channels), F32),
        pltpu.VMEM((tokens, channels), F32),
        pltpu.VMEM((GROUP, PACK * CELLS), BF16),
        pltpu.VMEM((PACK * CELLS, GROUP), BF16),
        last_mask,
        *[pltpu.VMEM(w.shape, F32) for w in weights],
        *[pltpu.VMEM(w.shape, BF16) for w in weights for _ in range(2)],
        pltpu.SemaphoreType.DMA((4,)),
    ]


PARAMS = dict(vmem_limit_bytes=58 * 1024 * 1024)


def whole(array):
    return pl.BlockSpec(array.shape, lambda i: (0,) * array.ndim)


def cost(tokens, channels, hidden):
    flops = 2 * 3 * tokens * channels * (4 * channels + 2 * hidden)
    return pl.CostEstimate(
        flops=2 * flops, bytes_accessed=8 * tokens * channels, transcendentals=tokens * hidden
    )


def spatial_call(plans, steps, gains, weights, after=()):
    cols, channels = plans[0][0][0][1].shape[1:]
    counts = [[len(arrays) for arrays, _ in plan] for plan in plans]
    hidden = weights[2].shape[1]
    in_specs, operands = [], []
    for plan in plans:
        for arrays, index in plan:
            for array in arrays:
                in_specs.append(
                    pl.BlockSpec((HALF,) + array.shape[1:], lambda i, index=index: (index(i), 0, 0))
                )
                operands.append(array)
    in_specs += [whole(gain) for gain in gains]
    in_specs += [pl.BlockSpec(memory_space=pl.ANY)] * (4 + len(after))
    bands = max(len(plan) for plan in plans) // 2
    ones = pltpu.VMEM((2 * bands - 1, 3, PACK * CELLS, GROUP), BF16)
    tokens = bands * WIN * (cols + WIN)
    return pl.pallas_call(
        functools.partial(spatial_kernel, counts, len(after)),
        grid=(steps,),
        in_specs=in_specs,
        out_specs=pl.BlockSpec((WIN, 1, cols, channels), lambda i: (0, i, 0, 0)),
        out_shape=jax.ShapeDtypeStruct((WIN, steps, cols, channels), F32),
        scratch_shapes=scratch(tokens, ones, weights),
        compiler_params=pltpu.CompilerParams(**PARAMS),
        cost_estimate=cost(steps * WIN * cols, channels, hidden),
        name="spatial",
    )(*operands, *gains, *weights, *after)


def temporal_call(x, gains, weights, after=(), cells=64):
    frames, count, channels = x.shape
    hidden = weights[2].shape[1]
    block = pl.BlockSpec((frames, cells, channels), lambda i: (0, i, 0))
    causal = pltpu.VMEM((CELLS, PACK * CELLS), F32)
    return pl.pallas_call(
        functools.partial(temporal_kernel, len(after)),
        grid=(count // cells,),
        in_specs=[block, *[whole(g) for g in gains]] + [pl.BlockSpec(memory_space=pl.ANY)] * (4 + len(after)),
        out_specs=block,
        out_shape=jax.ShapeDtypeStruct(x.shape, F32),
        scratch_shapes=scratch(frames * cells, causal, weights),
        compiler_params=pltpu.CompilerParams(**PARAMS),
        cost_estimate=cost(frames * count, channels, hidden),
        name="temporal",
    )(x, *gains, *weights, *after)


def exchange(x):
    return lax.all_to_all(x, "tm", split_axis=0, concat_axis=0, tiled=True)


def neighbours(high_edge, low_edge, axis):
    count = lax.axis_size(axis)
    forward = [(i, i + 1) for i in range(count - 1)]
    backward = [(target, source) for source, target in forward]
    return lax.ppermute(high_edge, axis, forward), lax.ppermute(low_edge, axis, backward)


def per_device(
    tokens,
    spatial_norm,
    spatial_qkv,
    spatial_out,
    spatial_mlpnorm,
    spatial_up,
    spatial_down,
    temporal_norm,
    temporal_qkv,
    temporal_out,
    temporal_mlpnorm,
    temporal_up,
    temporal_down,
):
    _, row_n, col_n, channels = tokens.shape
    tokens = tokens.reshape(row_n, col_n, channels)
    left, right = neighbours(tokens[:, -WIN:], tokens[:, :WIN], "col")
    def widened(cut):
        return jnp.concatenate([left[cut], tokens[cut], right[cut]], axis=1)

    above, below = neighbours(widened(slice(-HALF, None)), widened(slice(HALF)), "row")
    s_weights = (spatial_qkv, spatial_out, spatial_up, spatial_down)
    t_weights = (temporal_qkv, temporal_out, temporal_up, temporal_down)
    s_gains = (spatial_norm, spatial_mlpnorm)
    t_gains = (temporal_norm, temporal_mlpnorm)
    near = (left, tokens, right)
    last = row_n // HALF - 1
    inner = row_n // WIN - 1
    early = inner - 1

    def strip(first):
        return [(near, lambda i: 2 * (i + first) + 1), (near, lambda i: 2 * (i + first) + 2)]

    late = [(near, lambda i: 2 * early + 1), (near, lambda i: 2 * early + 2)]
    edge = [
        ((above,), lambda i: 0),
        (near, lambda i: 0),
        (near, lambda i: last),
        ((below,), lambda i: 0),
    ]
    early_piece = spatial_call([strip(0)], early, s_gains, s_weights)
    late_piece = spatial_call([late, edge], 2, s_gains, s_weights, (early_piece,))
    results, before = [], ()
    for piece in (early_piece, late_piece):
        arrived = exchange(piece.reshape(WIN, -1, channels))
        done = temporal_call(arrived, t_gains, t_weights, before)
        before = (done,)
        results.append(exchange(done).reshape(piece.shape))
    inner_rows = results[0].transpose(1, 0, 2, 3).reshape(-1, col_n, channels)
    strip_rows, edges = results[1][:, 0], results[1][:, 1]
    outcome = jnp.pad(inner_rows, ((HALF, row_n - HALF - inner_rows.shape[0]), (0, 0), (0, 0)))
    outcome = lax.dynamic_update_slice(outcome, strip_rows, (HALF + early * WIN, 0, 0))
    outcome = lax.dynamic_update_slice(outcome, edges[:HALF], (0, 0, 0))
    outcome = lax.dynamic_update_slice(outcome, edges[HALF:], (row_n - HALF, 0, 0))
    return outcome.reshape(1, row_n, col_n, channels)


def solution(mesh):
    placed = (P("tm", "row", "col", None),) + (P(),) * 12
    return jax.shard_map(
        per_device,
        mesh=mesh,
        in_specs=placed,
        out_specs=P("tm", "row", "col", None),
        check_vma=False,
    )
```

```python
import functools
import math

import jax
import jax.numpy as jnp
from jax import lax
from jax.experimental import pallas as pl
from jax.experimental.pallas import tpu as pltpu
from jax.sharding import PartitionSpec as P

HDIM = 32
WIN = 8
HALF = WIN // 2
EPSILON = 1e-05
SOFTCAP = 20.0
GROUP = 128
PACK = GROUP // HDIM
CELLS = WIN * WIN
SCORE_SCALE = 1.0 / (SOFTCAP * math.sqrt(HDIM))
EXP_SCALE = SOFTCAP * math.log2(math.e)
GELU_A = math.sqrt(2.0 / math.pi)
GELU_B = 0.044715 * GELU_A
BF16 = jnp.bfloat16
F32 = jnp.float32
F8 = jnp.float8_e4m3fn


def halves(value):
    high = value.astype(BF16)
    low = (value - high.astype(F32)).astype(BF16)
    return high, low


def dot(left, right, contract=((1,), (0,))):
    return lax.dot_general(left, right, (contract, ((), ())), preferred_element_type=F32)


def dot3(value, weight_high, weight_low):
    high, low = halves(value)
    left = jnp.concatenate([high, low, high], axis=1)
    right = jnp.concatenate([weight_high, weight_high, weight_low], axis=0)
    return dot(left, right)


def dot_small(value, weight_high, weight_low):
    high = value.astype(BF16)
    rest = (value - high.astype(F32)) * 512.0
    left = jnp.concatenate([rest.astype(F8), high.astype(F32).astype(F8)], axis=1)
    lower = (weight_low.astype(F32) * (512.0 * 256.0)).astype(F8)
    upper = (weight_high.astype(F32) * 256.0).astype(F8)
    correction = dot(left, jnp.concatenate([upper, lower], axis=0))
    return dot(high, weight_high) + correction * (1.0 / (512.0 * 256.0))


def layer_norm(inputs, scales):
    average = jnp.mean(inputs, axis=-1, keepdims=True)
    centred = inputs - average
    spread = jnp.mean(centred * centred, axis=-1, keepdims=True)
    return centred * lax.rsqrt(spread + EPSILON) * scales


def gelu(x):
    return 0.5 * x * (1.0 + jnp.tanh(x * (GELU_A + GELU_B * (x * x))))


def fold(stacked):
    return stacked[:CELLS] + stacked[CELLS:]


def attend_tile(qkv, mix, row0, key_mask, value_mask, ones_block, score_mask):
    channels = mix.shape[-1]
    rows = pl.ds(row0, CELLS)
    for group in range(channels // GROUP):
        lanes = group * GROUP

        def part(index):
            return qkv[rows, index * channels + lanes : index * channels + lanes + GROUP]

        q_high, q_low = halves(part(0) * SCORE_SCALE)
        keys = part(1)
        k_high, k_low = halves(jnp.concatenate([keys, keys], axis=0).T)
        v_high, v_low = halves(part(2))

        def key_block(tile):
            return jnp.concatenate([tile] * (PACK // 2), axis=1) * key_mask[...]

        def value_block(tile):
            return jnp.concatenate([tile] * PACK, axis=0) * value_mask[...]

        left = jnp.concatenate([q_high, q_low], axis=0)
        right = jnp.concatenate([key_block(k_high), key_block(k_low)], axis=1)
        scores = fold(dot(left, right))
        scores = scores[:, : PACK * CELLS] + scores[:, PACK * CELLS :]
        weights = jnp.exp2(EXP_SCALE * jnp.tanh(scores))
        if score_mask is not None:
            weights = weights * score_mask[...]
        left = jnp.concatenate(halves(weights), axis=0)
        right = jnp.concatenate([value_block(v_high), ones_block, value_block(v_low)], axis=1)
        summed = fold(dot(left, right))
        total = summed[:, :GROUP] + summed[:, 2 * GROUP :]
        mix[rows, lanes : lanes + GROUP] = total / summed[:, GROUP : 2 * GROUP]


def finish(stream, mixture, w_out, gain, w_up, w_down, small=False, chunk=512):
    stream = stream + dot3(mixture, *[w[...] for w in w_out])
    normed = layer_norm(stream, gain[...])
    n_high, n_low = halves(normed)
    left = jnp.concatenate([n_high, n_low, n_high], axis=1)
    up_high, up_low = w_up
    down_high, down_low = w_down
    total = stream
    for start in range(0, up_high.shape[1], chunk):
        cut = slice(start, start + chunk)
        right = jnp.concatenate([up_high[:, cut], up_high[:, cut], up_low[:, cut]], axis=0)
        hidden = gelu(dot(left, right))
        if small:
            total = total + dot_small(hidden, down_high[cut, :], down_low[cut, :])
        else:
            total = total + dot3(hidden, down_high[cut, :], down_low[cut, :])
    return total


class Weights:
    def __init__(self, sources, staged, buffers, semaphores):
        self.sources, self.staged, self.buffers = sources, staged, buffers
        self.copies = [
            pltpu.make_async_copy(source, stage, semaphores.at[i])
            for i, (source, stage) in enumerate(zip(sources, staged))
        ]
        self.pairs = [buffers[i : i + 2] for i in range(0, 8, 2)]

    def start(self):
        for copy in self.copies:
            copy.start()

    def split(self, first, last, block=64):
        for i in range(first, last):
            self.copies[i].wait()
            stage, (high, low) = self.staged[i], self.pairs[i]

            @pl.loop(0, stage.shape[0] // block)
            def _(step):
                rows = pl.ds(pl.multiple_of(step * block, block), block)
                high[rows, :], low[rows, :] = halves(stage[rows, :])


def iota(shape, dim):
    return lax.broadcasted_iota(jnp.int32, shape, dim)


def as_mask(condition, dtype=BF16):
    return jnp.where(condition, 1.0, 0.0).astype(dtype)


def block_masks(key_mask, value_mask):
    shape = (GROUP, PACK * CELLS)
    key_mask[...] = as_mask(iota(shape, 0) // HDIM == iota(shape, 1) // CELLS)
    shape = shape[::-1]
    block = iota(shape, 0) // CELLS == iota(shape, 1) // HDIM
    value_mask[...] = as_mask(block)
    return block


def spatial_kernel(plans, after, *refs):
    tile_count = sum(sum(plan) for plan in plans)
    tiles, refs = refs[:tile_count], refs[tile_count:]
    gain_attn, gain_mlp = refs[:2]
    sources, refs = refs[2:6], refs[6 + after :]
    out, qkv, mix, key_mask, value_mask, ones = refs[:6]
    weights = Weights(sources, refs[6:10], refs[10:18], refs[18])
    w_qkv, w_out, w_up, w_down = weights.pairs
    step = pl.program_id(0)
    cols, channels = out.shape[2], mix.shape[-1]
    lane_tiles = cols // WIN
    windows = lane_tiles + 1
    tokens = windows * CELLS

    @pl.when(step == 0)
    def _():
        weights.start()
        block = block_masks(key_mask, value_mask)
        key = iota((PACK * CELLS, GROUP), 0) % CELLS
        key_row, key_col = key // WIN, key % WIN
        row, row_last = lax.axis_index("row"), lax.axis_size("row") - 1
        col, col_last = lax.axis_index("col"), lax.axis_size("col") - 1
        col_ok = [
            key_col < jnp.where(col > 0, WIN, HALF),
            key_col >= 0,
            key_col >= jnp.where(col < col_last, 0, HALF),
        ]
        row_ok = [
            key_row >= 0,
            key_row >= jnp.where(row > 0, 0, HALF),
            key_row < jnp.where(row < row_last, WIN, HALF),
        ]
        for i in range(ones.shape[0]):
            for j in range(3):
                ones[i, j] = as_mask(block & row_ok[i] & col_ok[j])
        weights.split(0, 1)

    upper = iota((1, 1, WIN, channels), 2) >= HALF

    def run(pieces):
        bands = len(pieces) // 2
        for band in range(bands):
            parts = []
            for piece in pieces[2 * band : 2 * band + 2]:
                parts.append(
                    jnp.concatenate([t[...].reshape(HALF, -1, WIN, channels) for t in piece], axis=1)
                )
            wide = jnp.concatenate(parts, axis=0)
            wide = jnp.where(upper, wide[:, :windows], wide[:, 1:]).transpose(1, 0, 2, 3)
            normed = layer_norm(wide.reshape(tokens, channels), gain_attn[...])
            projected = dot3(normed, w_qkv[0][...], w_qkv[1][...])
            qkv[band * tokens : (band + 1) * tokens, :] = projected
        for band in range(bands):
            kind = 0 if bands == 1 else band + 1

            def window(j, carry, band=band, kind=kind):
                edge = jnp.where(j == 0, 0, jnp.where(j == windows - 1, 2, 1))
                row0 = pl.multiple_of(band * tokens + j * CELLS, CELLS)
                attend_tile(qkv, mix, row0, key_mask, value_mask, ones[kind, edge], None)
                return carry

            lax.fori_loop(0, windows, window, 0, unroll=9)

        @pl.when(step == 0)
        def _():
            weights.split(1, 4)

        if bands == 1:
            stream = jnp.concatenate([piece[1][...] for piece in pieces], axis=0)
            blended = mix[:tokens, :].reshape(windows, WIN, WIN, channels)
        else:
            stream = jnp.concatenate([piece[1][...] for piece in pieces[1:3]], axis=0)
            first = mix[:tokens, :].reshape(windows, WIN, WIN, channels)
            second = mix[tokens:, :].reshape(windows, WIN, WIN, channels)
            blended = jnp.concatenate([first[:, HALF:], second[:, :HALF]], axis=1)
        blended = jnp.where(upper, blended[1:], blended[:lane_tiles])
        stream = stream.reshape(WIN, lane_tiles, WIN, channels).transpose(1, 0, 2, 3)
        result = finish(
            stream.reshape(WIN * cols, channels),
            blended.reshape(WIN * cols, channels),
            w_out,
            gain_mlp,
            w_up,
            w_down,
        )
        result = result.reshape(lane_tiles, WIN, WIN, channels).transpose(1, 0, 2, 3)
        out[...] = result.reshape(out.shape)

    at = 0
    for i, plan in enumerate(plans):
        pieces = []
        for count in plan:
            pieces.append(tiles[at : at + count])
            at += count
        if len(plans) == 1:
            run(pieces)
        else:
            pl.when(step == i)(functools.partial(run, pieces))


def temporal_kernel(after, x, gain_attn, gain_mlp, *refs):
    sources, refs = refs[:4], refs[4 + after :]
    out, qkv, mix, key_mask, value_mask, causal = refs[:6]
    weights = Weights(sources, refs[6:10], refs[10:18], refs[18])
    w_qkv, w_out, w_up, w_down = weights.pairs
    first = pl.program_id(0) == 0
    frames, cells, channels = x.shape
    groups = cells // WIN

    @pl.when(first)
    def _():
        weights.start()
        block_masks(key_mask, value_mask)
        query, key = iota(causal.shape, 0), iota(causal.shape, 1) % CELLS
        same = query % WIN == key % WIN
        causal[...] = as_mask(same & (key // WIN <= query // WIN), F32)
        weights.split(0, 1)

    stream = x[...].reshape(frames, groups, WIN, channels).transpose(1, 0, 2, 3)
    stream = stream.reshape(frames * cells, channels)
    normed = layer_norm(stream, gain_attn[...])
    qkv[...] = dot3(normed, w_qkv[0][...], w_qkv[1][...])

    def cell_group(j, carry):
        row0 = pl.multiple_of(j * CELLS, CELLS)
        attend_tile(qkv, mix, row0, key_mask, value_mask, value_mask[...], causal)
        return carry

    lax.fori_loop(0, groups, cell_group, 0, unroll=8)

    @pl.when(first)
    def _():
        weights.split(1, 4)

    result = finish(stream, mix[...], w_out, gain_mlp, w_up, w_down, small=True)
    result = result.reshape(groups, frames, WIN, channels).transpose(1, 0, 2, 3)
    out[...] = result.reshape(out.shape)


def scratch(tokens, last_mask, weights):
    channels = weights[1].shape[0]
    return [
        pltpu.VMEM((tokens, 3 * channels), F32),
        pltpu.VMEM((tokens, channels), F32),
        pltpu.VMEM((GROUP, PACK * CELLS), BF16),
        pltpu.VMEM((PACK * CELLS, GROUP), BF16),
        last_mask,
        *[pltpu.VMEM(w.shape, F32) for w in weights],
        *[pltpu.VMEM(w.shape, BF16) for w in weights for _ in range(2)],
        pltpu.SemaphoreType.DMA((4,)),
    ]


PARAMS = dict(vmem_limit_bytes=58 * 1024 * 1024)


def whole(array):
    return pl.BlockSpec(array.shape, lambda i: (0,) * array.ndim)


def cost(tokens, channels, hidden):
    flops = 2 * 3 * tokens * channels * (4 * channels + 2 * hidden)
    return pl.CostEstimate(
        flops=2 * flops, bytes_accessed=8 * tokens * channels, transcendentals=tokens * hidden
    )


def spatial_call(plans, steps, gains, weights, after=()):
    cols, channels = plans[0][0][0][1].shape[1:]
    counts = [[len(arrays) for arrays, _ in plan] for plan in plans]
    hidden = weights[2].shape[1]
    in_specs, operands = [], []
    for plan in plans:
        for arrays, index in plan:
            for array in arrays:
                in_specs.append(
                    pl.BlockSpec((HALF,) + array.shape[1:], lambda i, index=index: (index(i), 0, 0))
                )
                operands.append(array)
    in_specs += [whole(gain) for gain in gains]
    in_specs += [pl.BlockSpec(memory_space=pl.ANY)] * (4 + len(after))
    bands = max(len(plan) for plan in plans) // 2
    ones = pltpu.VMEM((2 * bands - 1, 3, PACK * CELLS, GROUP), BF16)
    tokens = bands * WIN * (cols + WIN)
    return pl.pallas_call(
        functools.partial(spatial_kernel, counts, len(after)),
        grid=(steps,),
        in_specs=in_specs,
        out_specs=pl.BlockSpec((WIN, 1, cols, channels), lambda i: (0, i, 0, 0)),
        out_shape=jax.ShapeDtypeStruct((WIN, steps, cols, channels), F32),
        scratch_shapes=scratch(tokens, ones, weights),
        compiler_params=pltpu.CompilerParams(**PARAMS),
        cost_estimate=cost(steps * WIN * cols, channels, hidden),
        name="spatial",
    )(*operands, *gains, *weights, *after)


def temporal_call(x, gains, weights, after=(), cells=64):
    frames, count, channels = x.shape
    hidden = weights[2].shape[1]
    block = pl.BlockSpec((frames, cells, channels), lambda i: (0, i, 0))
    causal = pltpu.VMEM((CELLS, PACK * CELLS), F32)
    return pl.pallas_call(
        functools.partial(temporal_kernel, len(after)),
        grid=(count // cells,),
        in_specs=[block, *[whole(g) for g in gains]] + [pl.BlockSpec(memory_space=pl.ANY)] * (4 + len(after)),
        out_specs=block,
        out_shape=jax.ShapeDtypeStruct(x.shape, F32),
        scratch_shapes=scratch(frames * cells, causal, weights),
        compiler_params=pltpu.CompilerParams(**PARAMS),
        cost_estimate=cost(frames * count, channels, hidden),
        name="temporal",
    )(x, *gains, *weights, *after)


def exchange(x):
    return lax.all_to_all(x, "tm", split_axis=0, concat_axis=0, tiled=True)


def neighbours(high_edge, low_edge, axis):
    count = lax.axis_size(axis)
    forward = [(i, i + 1) for i in range(count - 1)]
    backward = [(target, source) for source, target in forward]
    return lax.ppermute(high_edge, axis, forward), lax.ppermute(low_edge, axis, backward)


def per_device(
    tokens,
    spatial_norm,
    spatial_qkv,
    spatial_out,
    spatial_mlpnorm,
    spatial_up,
    spatial_down,
    temporal_norm,
    temporal_qkv,
    temporal_out,
    temporal_mlpnorm,
    temporal_up,
    temporal_down,
):
    _, row_n, col_n, channels = tokens.shape
    tokens = tokens.reshape(row_n, col_n, channels)
    left, right = neighbours(tokens[:, -WIN:], tokens[:, :WIN], "col")
    def widened(cut):
        return jnp.concatenate([left[cut], tokens[cut], right[cut]], axis=1)

    above, below = neighbours(widened(slice(-HALF, None)), widened(slice(HALF)), "row")
    s_weights = (spatial_qkv, spatial_out, spatial_up, spatial_down)
    t_weights = (temporal_qkv, temporal_out, temporal_up, temporal_down)
    s_gains = (spatial_norm, spatial_mlpnorm)
    t_gains = (temporal_norm, temporal_mlpnorm)
    near = (left, tokens, right)
    last = row_n // HALF - 1
    inner = row_n // WIN - 1
    early = inner - 1

    def strip(first):
        return [(near, lambda i: 2 * (i + first) + 1), (near, lambda i: 2 * (i + first) + 2)]

    late = [(near, lambda i: 2 * early + 1), (near, lambda i: 2 * early + 2)]
    edge = [
        ((above,), lambda i: 0),
        (near, lambda i: 0),
        (near, lambda i: last),
        ((below,), lambda i: 0),
    ]
    early_piece = spatial_call([strip(0)], early, s_gains, s_weights)
    late_piece = spatial_call([late, edge], 2, s_gains, s_weights, (early_piece,))
    results, before = [], ()
    for piece in (early_piece, late_piece):
        arrived = exchange(piece.reshape(WIN, -1, channels))
        done = temporal_call(arrived, t_gains, t_weights, before)
        before = (done,)
        results.append(exchange(done).reshape(piece.shape))
    inner_rows = results[0].transpose(1, 0, 2, 3).reshape(-1, col_n, channels)
    strip_rows, edges = results[1][:, 0], results[1][:, 1]
    outcome = jnp.pad(inner_rows, ((HALF, row_n - HALF - inner_rows.shape[0]), (0, 0), (0, 0)))
    outcome = lax.dynamic_update_slice(outcome, strip_rows, (HALF + early * WIN, 0, 0))
    outcome = lax.dynamic_update_slice(outcome, edges[:HALF], (0, 0, 0))
    outcome = lax.dynamic_update_slice(outcome, edges[HALF:], (row_n - HALF, 0, 0))
    return outcome.reshape(1, row_n, col_n, channels)


def solution(mesh):
    placed = (P("tm", "row", "col", None),) + (P(),) * 12
    return jax.shard_map(
        per_device,
        mesh=mesh,
        in_specs=placed,
        out_specs=P("tm", "row", "col", None),
        check_vma=False,
    )
```
